128 devices in a mesh: genome: 64 (over x, z, y_hi, core), sample: 2 (over y_lo).
Axes of the slice: x: 4, y: 4 (y_hi: 2, y_lo: 2; y = y_hi * 2 + y_lo), z: 4, core: 2. Of those that a mesh axis runs over, the one named last changes fastest.
Arguments:
- dosage: bfloat16 [512, 262144], P(('genome', 'sample'))
- missing: int32 [262144], replicated, may hold values from 0 to 128
- positions: int32 [262144], replicated, may hold values from 0 to 512, as said below
- chrom_end: int32 [262144], replicated, may hold values 0 or 1
- pair_pattern: int32 [1024, 5], replicated, may hold values 0 or 1
Outputs:
- ld: bfloat16 [262144, 1280], P(('genome', 'sample'))
The draws below stay inside these ranges and needn't reach their ends.
Inputs may be any that keep to these rules, and one draw needn't show every extreme that they name: positions start at 0 and never fall; from one variant to the next they rise by 0 or 1.
All inputs are finite; a program needn't handle non-finite values.
Results may differ from the reference program's by a relative error of at most 0.0026.
Values may be sent and summed in bfloat16 or wider, within the bound.
No kernel may reach another device: no remote copies, remote signals or barrier semaphores. Data moves between devices by JAX's collectives and lax.ppermute only.
A program may use at most 192 MiB of HBM per device.

```python
import jax
import jax.numpy as jnp
from jax import lax

SAMPLES = 512
BLK = 256
BAND = 4
VARIANTS = 262144
NBLOCKS = 1024


def draw_dosage(key, part):
    key = jax.random.fold_in(key, 11)
    key_near, key_far, key_noise = jax.random.split(key, 3)
    near = jax.random.normal(key_near, (SAMPLES, VARIANTS // 32), jnp.float32)
    far = jax.random.normal(key_far, (SAMPLES, VARIANTS // 512), jnp.float32)
    noise = jax.random.normal(key_noise, (SAMPLES, VARIANTS), jnp.float32)
    values = 0.8 * noise + 0.6 * jnp.repeat(near, 32, axis=1) + 0.4 * jnp.repeat(far, 512, axis=1)
    values = values + 1.0
    return values.astype(jnp.bfloat16)


def draw_positions(key, part):
    key = jax.random.fold_in(key, 23)
    rises = VARIANTS // (2 * BLK)
    order = jax.random.permutation(key, VARIANTS - 1)
    steps = (order < rises).astype(jnp.int32)
    steps = jnp.concatenate([jnp.zeros((1,), jnp.int32), steps])
    return jnp.cumsum(steps).astype(jnp.int32)


def with_ends(result, own_key, low, high):
    longest = result.shape.index(max(result.shape))
    spots = []
    for shift in (0, 1):
        where = [jax.random.randint(jax.random.fold_in(own_key, axis), (), 0, length) for axis, length in enumerate(result.shape)]
        where[longest] = (where[longest] + shift) % result.shape[longest]
        spots.append(tuple(where))
    return result.at[spots[0]].set(low).at[spots[1]].set(high)


def setup_inputs(seed: int = 0) -> dict:
    keys = jax.random.split(jax.random.key(seed), 6)
    dosage = draw_dosage(jax.random.fold_in(keys[5], 71), 0)
    missing = with_ends(jax.random.randint(keys[1], (VARIANTS,), 0, SAMPLES // 4 + 1), jax.random.fold_in(keys[1], 1), 0, (SAMPLES // 4 + 1) - 1).astype(jnp.int32)
    positions = draw_positions(jax.random.fold_in(keys[5], 71), 0)
    chrom_end = with_ends((jax.random.randint(keys[3], (VARIANTS,), 0, 8 * BLK) < 1).astype(jnp.int32), jax.random.fold_in(keys[3], 1), 0, 1)
    pair_pattern = with_ends((jax.random.randint(keys[4], (NBLOCKS, BAND + 1), 0, 4) < 3).astype(jnp.int32), jax.random.fold_in(keys[4], 1), 0, 1)
    return dict(dosage=dosage, missing=missing, positions=positions, chrom_end=chrom_end, pair_pattern=pair_pattern)


def reference(dosage, missing, positions, chrom_end, pair_pattern):
    count = (SAMPLES - missing).astype(jnp.float32)
    values = dosage.astype(jnp.float32)
    mean = lax.optimization_barrier(jnp.sum(values, axis=0)) / count
    centred = values - mean[None, :]
    var = lax.optimization_barrier(jnp.sum(centred * centred, axis=0)) / count
    zvals = (centred / jnp.sqrt(var + 1e-05)[None, :]).astype(jnp.bfloat16)
    seg = jnp.cumsum(chrom_end).astype(jnp.int32) - chrom_end
    scale = 1.0 / jnp.sqrt(count)
    rim = BAND * BLK
    zpad = jnp.concatenate([zvals, jnp.zeros((SAMPLES, rim), jnp.bfloat16)], axis=1)
    pos_pad = jnp.concatenate([positions, jnp.full((rim,), -4, jnp.int32)])
    seg_pad = jnp.concatenate([seg, jnp.full((rim,), -1, jnp.int32)])
    scale_pad = jnp.concatenate([scale, jnp.zeros((rim,), jnp.float32)])
    width = (BAND + 1) * BLK

    def one_block(block):
        first = (block * BLK).astype(jnp.int32)
        rows = lax.dynamic_slice_in_dim(zvals, first, BLK, 1)
        cols = lax.dynamic_slice_in_dim(zpad, first, width, 1)
        prod = jnp.dot(rows.T, cols, preferred_element_type=jnp.float32)
        pos_r = lax.dynamic_slice_in_dim(positions, first, BLK, 0)
        pos_c = lax.dynamic_slice_in_dim(pos_pad, first, width, 0)
        seg_r = lax.dynamic_slice_in_dim(seg, first, BLK, 0)
        seg_c = lax.dynamic_slice_in_dim(seg_pad, first, width, 0)
        sca_r = lax.dynamic_slice_in_dim(scale, first, BLK, 0)
        sca_c = lax.dynamic_slice_in_dim(scale_pad, first, width, 0)
        patt = lax.dynamic_slice_in_dim(pair_pattern, block.astype(jnp.int32), 1, 0)[0]
        patt_cols = jnp.repeat(patt, BLK)
        keep = (jnp.abs(pos_r[:, None] - pos_c[None, :]) <= 1) & (seg_r[:, None] == seg_c[None, :]) & (patt_cols[None, :] == 1)
        return jnp.where(keep, prod * (sca_r[:, None] * sca_c[None, :]), 0.0).astype(jnp.bfloat16)
    out = lax.map(one_block, jnp.arange(NBLOCKS, dtype=jnp.int32))
    return out.reshape(VARIANTS, width)
```

```python
import jax
import jax.numpy as jnp
from jax import lax
from jax.experimental import pallas as pl
from jax.experimental.pallas import tpu as pltpu
from jax.sharding import PartitionSpec as P

SAMPLES = 512
BLK = 256
BAND = 4
RIM = BAND * BLK
WIDTH = RIM + BLK
AXES = ("genome", "sample")
FAR = 1e9


def standardize(dosage_ref, count_ref, z_ref, block):
    cols = pl.ds(pl.multiple_of(block * BLK, BLK), BLK)
    values = dosage_ref[:, :, cols].astype(jnp.float32).reshape(SAMPLES, BLK)
    count = count_ref[block]
    mean = jnp.sum(values, axis=0, keepdims=True) / count
    centred = values - mean
    var = jnp.sum(centred * centred, axis=0, keepdims=True) / count
    z_ref[block] = (centred * (1.0 / jnp.sqrt(var + 1e-05))).astype(jnp.bfloat16)


def band_kernel(dosage_ref, count_ref, key_row_ref, scale_row_ref, key_col_ref, scale_col_ref, ld_ref, z_ref):
    i = pl.program_id(0)

    @pl.when(i == 0)
    def _():
        @pl.loop(0, BAND + 1)
        def _(block):
            standardize(dosage_ref, count_ref, z_ref, block)

    @pl.when(i < pl.num_programs(0) - 1)
    def _():
        standardize(dosage_ref, count_ref, z_ref, i + BAND + 1)

    left = z_ref[i].T
    key_a = key_col_ref[...]
    scale_a = scale_col_ref[...]
    for offset in range(BAND + 1):
        prod = jnp.dot(left, z_ref[i + offset], preferred_element_type=jnp.float32)
        for half in range(2):
            first = offset * BLK + half * 128
            key_j = key_row_ref[0, :, first : first + 128]
            scale_j = scale_row_ref[0, :, first : first + 128]
            keep = key_j <= key_a + 1.0
            if offset == 0:
                keep &= key_j >= key_a - 1.0
            ld = jnp.where(keep, prod[:, half * 128 : half * 128 + 128] * (scale_a * scale_j), 0.0)
            ld_ref[:, first : first + 128] = ld.astype(jnp.bfloat16)


def on_device(dosage, missing, positions, chrom_end, pair_pattern):
    nvar_all = dosage.shape[1]
    ndev = lax.axis_size("genome") * lax.axis_size("sample")
    nvar = nvar_all // ndev
    nblk = nvar // BLK
    slab = lax.axis_index(AXES)
    row_first = slab * nvar
    last = slab == ndev - 1

    blocks = dosage.reshape(-1, ndev, nvar).transpose(1, 0, 2)
    rim = jnp.concatenate([blocks[1:, :, :RIM], jnp.zeros_like(blocks[:1, :, :RIM])], axis=0)
    mine = lax.all_to_all(
        jnp.concatenate([blocks, rim], axis=2), AXES, split_axis=0, concat_axis=0, tiled=True
    )

    def extended(table, fill):
        own = lax.dynamic_slice_in_dim(table, row_first, nvar, 0)
        start = jnp.minimum(row_first + nvar, nvar_all - RIM)
        after = lax.dynamic_slice_in_dim(table, start, RIM, 0)
        return jnp.concatenate([own, jnp.where(last, fill, after)])

    count = (SAMPLES - extended(missing, 0)).astype(jnp.float32)
    ends = extended(chrom_end, 0)
    seg = jnp.cumsum(ends) - ends
    key = (extended(positions, 0) + 4 * seg).astype(jnp.float32)
    key = jnp.where(last & (jnp.arange(nvar + RIM) >= nvar), FAR, key)
    scale = 1.0 / jnp.sqrt(count)

    def window(table):
        grid = table.reshape(-1, BLK)
        return jnp.stack([grid[k : k + nblk] for k in range(BAND + 1)], axis=1)

    pattern = lax.dynamic_slice_in_dim(pair_pattern, slab * nblk, nblk, 0)
    key_row = jnp.where(pattern[:, :, None] == 1, window(key), FAR).reshape(nblk, 1, WIDTH)
    scale_row = window(scale).reshape(nblk, 1, WIDTH)
    key_col = jnp.broadcast_to(key[:nvar, None], (nvar, 128))
    scale_col = jnp.broadcast_to(scale[:nvar, None], (nvar, 128))

    whole = pl.BlockSpec(memory_space=pltpu.VMEM)
    row_spec = pl.BlockSpec((1, 1, WIDTH), lambda i: (i, 0, 0))
    col_spec = pl.BlockSpec((BLK, 128), lambda i: (i, 0))
    return pl.pallas_call(
        band_kernel,
        grid=(nblk,),
        in_specs=[whole, whole, row_spec, row_spec, col_spec, col_spec],
        out_specs=pl.BlockSpec((BLK, WIDTH), lambda i: (i, 0)),
        out_shape=jax.ShapeDtypeStruct((nvar, WIDTH), jnp.bfloat16),
        scratch_shapes=[pltpu.VMEM((nblk + BAND, SAMPLES, BLK), jnp.bfloat16)],
        compiler_params=pltpu.CompilerParams(vmem_limit_bytes=40 << 20),
    )(mine, count.reshape(-1, 1, BLK), key_row, scale_row, key_col, scale_col)


def solution(mesh):
    placed = (P(AXES, None), P(), P(), P(), P())
    return jax.shard_map(
        on_device,
        mesh=mesh,
        in_specs=placed,
        out_specs=P(AXES, None),
        check_vma=False,
    )
```

```python
import jax
import jax.numpy as jnp
from jax import lax
from jax.experimental import pallas as pl
from jax.experimental.pallas import tpu as pltpu
from jax.sharding import PartitionSpec as P

SAMPLES = 512
BLK = 256
BAND = 4
RIM = BAND * BLK
WIDTH = RIM + BLK
CHUNK = 64
PACKS = 4
AXES = ("genome", "sample")
FAR = 1e9


def pack_kernel(slabs_ref, sent_ref, held_ref, sem):
    ndev, _, nvar = slabs_ref.shape
    step = ndev // PACKS
    first, own, edge = pl.ds(0, RIM), pl.ds(0, nvar), pl.ds(nvar, RIM)
    reads = [
        pltpu.make_async_copy(slabs_ref.at[part], held_ref.at[part], sem.at[0, p])
        for p, part in enumerate(pl.ds(p * step, step) for p in range(PACKS))
    ]
    for read in reads:
        read.start()
    writes = []
    for p, read in enumerate(reads):
        read.wait()
        part = pl.ds(p * step, step)
        writes.append(pltpu.make_async_copy(held_ref.at[part], sent_ref.at[part, :, own], sem.at[1, p]))
        low = max(p * step, 1)
        count = (p + 1) * step - low
        writes.append(
            pltpu.make_async_copy(
                held_ref.at[pl.ds(low, count), :, first], sent_ref.at[pl.ds(low - 1, count), :, edge], sem.at[2, p]
            )
        )
        if p == 0:
            writes.append(
                pltpu.make_async_copy(
                    held_ref.at[pl.ds(0, 1), :, first], sent_ref.at[pl.ds(ndev - 1, 1), :, edge], sem.at[3, 0]
                )
            )
        for write in writes[2 * p + (p > 0) :]:
            write.start()
    for write in writes:
        write.wait()


def standardize(dosage_ref, count_ref, z_ref, block):
    cols = slice(block * BLK, (block + 1) * BLK)
    step = CHUNK * dosage_ref.shape[0] // SAMPLES
    chunks = [slice(g * CHUNK, (g + 1) * CHUNK) for g in range(SAMPLES // CHUNK)]

    def total(parts):
        part = sum(p.reshape(CHUNK // 8, 8, BLK).sum(axis=0) for p in parts)
        return part.sum(axis=0, keepdims=True)

    def dosages():
        for g, rows in enumerate(chunks):
            values = dosage_ref[g * step : (g + 1) * step, :, cols].astype(jnp.float32).reshape(CHUNK, BLK)
            z_ref[block, rows, :] = values.astype(jnp.bfloat16)
            yield values

    def centred(rows):
        return z_ref[block, rows, :].astype(jnp.float32) - mean

    count = count_ref[block]
    mean = total(dosages()) / count
    var = total(c * c for c in map(centred, chunks)) / count
    inverse = 1.0 / jnp.sqrt(var + 1e-05)
    for rows in chunks:
        z_ref[block, rows, :] = (centred(rows) * inverse).astype(jnp.bfloat16)


def column(row):
    return jnp.broadcast_to(row, (128, row.shape[1])).T


def band_rows(z_ref, key_row_ref, scale_row_ref, key_own_ref, scale_own_ref, ld_ref, block):
    rows = slice(block * BLK, (block + 1) * BLK)
    left = z_ref[block].T
    top = column(key_own_ref[block] + 1.0)
    scale_a = column(scale_own_ref[block])
    for offset in range(BAND + 1):
        prod = jnp.dot(left, z_ref[block + offset], preferred_element_type=jnp.float32)
        for half in range(BLK // 128):
            cols = slice(offset * BLK + half * 128, offset * BLK + half * 128 + 128)
            key_j = key_row_ref[block, :, cols]
            keep = key_j <= top
            if offset == 0:
                keep &= key_j >= top - 2.0
            weight = scale_a * scale_row_ref[block, :, cols]
            ld = jnp.where(keep, prod[:, half * 128 : half * 128 + 128] * weight, 0.0)
            ld_ref[rows, cols] = ld.astype(jnp.bfloat16)


def band_kernel(
    dosage_ref, count_ref, key_row_ref, scale_row_ref, key_own_ref, scale_own_ref, out_ref, z_ref, ld_ref, sem
):
    nblk = key_row_ref.shape[0]
    copies = []
    for block in range(BAND + 1):
        standardize(dosage_ref, count_ref, z_ref, block)
    for block in range(nblk):
        if block + 1 < nblk:
            standardize(dosage_ref, count_ref, z_ref, block + BAND + 1)
        band_rows(z_ref, key_row_ref, scale_row_ref, key_own_ref, scale_own_ref, ld_ref, block)
        rows = pl.ds(block * BLK, BLK)
        copies.append(pltpu.make_async_copy(ld_ref.at[rows], out_ref.at[rows], sem.at[block]))
        copies[-1].start()
    for copy in copies:
        copy.wait()


def on_device(dosage, missing, positions, chrom_end, pair_pattern):
    nvar_all = dosage.shape[1]
    ndev = lax.axis_size("genome") * lax.axis_size("sample")
    nvar = nvar_all // ndev
    nblk = nvar // BLK
    slab = lax.axis_index(AXES)
    row_first = slab * nvar
    last = slab == ndev - 1

    slabs = dosage.reshape(-1, ndev, nvar).transpose(1, 0, 2)
    anywhere = pl.BlockSpec(memory_space=pl.ANY)
    sent = pl.pallas_call(
        pack_kernel,
        in_specs=[anywhere],
        out_specs=anywhere,
        out_shape=jax.ShapeDtypeStruct((ndev, slabs.shape[1], nvar + RIM), dosage.dtype),
        scratch_shapes=[pltpu.VMEM(slabs.shape, dosage.dtype), pltpu.SemaphoreType.DMA((4, PACKS))],
        compiler_params=pltpu.CompilerParams(vmem_limit_bytes=56 << 20),
    )(slabs)
    mine = lax.all_to_all(sent, AXES, split_axis=0, concat_axis=0, tiled=True)

    def extended(table, fill):
        own = lax.dynamic_slice_in_dim(table, row_first, nvar, 0)
        start = jnp.minimum(row_first + nvar, nvar_all - RIM)
        after = lax.dynamic_slice_in_dim(table, start, RIM, 0)
        return jnp.concatenate([own, jnp.where(last, fill, after)])

    count = (SAMPLES - extended(missing, 0)).astype(jnp.float32)
    ends = extended(chrom_end, 0)
    seg = jnp.cumsum(ends) - ends
    key = (extended(positions, 0) + 4 * seg).astype(jnp.float32)
    key = jnp.where(last & (jnp.arange(nvar + RIM) >= nvar), FAR, key)
    scale = 1.0 / jnp.sqrt(count)

    def window(table):
        grid = table.reshape(-1, BLK)
        return jnp.stack([grid[k : k + nblk] for k in range(BAND + 1)], axis=1)

    pattern = lax.dynamic_slice_in_dim(pair_pattern, slab * nblk, nblk, 0)
    key_row = jnp.where(pattern[:, :, None] == 1, window(key), FAR).reshape(nblk, 1, WIDTH)
    scale_row = window(scale).reshape(nblk, 1, WIDTH)
    key_own = key[:nvar].reshape(nblk, 1, BLK)
    scale_own = scale[:nvar].reshape(nblk, 1, BLK)

    whole = pl.BlockSpec(memory_space=pltpu.VMEM)
    return pl.pallas_call(
        band_kernel,
        in_specs=[whole] * 6,
        out_specs=anywhere,
        out_shape=jax.ShapeDtypeStruct((nvar, WIDTH), jnp.bfloat16),
        scratch_shapes=[
            pltpu.VMEM((nblk + BAND, SAMPLES, BLK), jnp.bfloat16),
            pltpu.VMEM((nvar, WIDTH), jnp.bfloat16),
            pltpu.SemaphoreType.DMA((nblk,)),
        ],
        compiler_params=pltpu.CompilerParams(vmem_limit_bytes=40 << 20),
    )(mine, count.reshape(-1, 1, BLK), key_row, scale_row, key_own, scale_own)


def solution(mesh):
    placed = (P(AXES, None), P(), P(), P(), P())
    return jax.shard_map(
        on_device,
        mesh=mesh,
        in_specs=placed,
        out_specs=P(AXES, None),
        check_vma=False,
    )
```
